32 devices in a mesh: ctx: 8 (over z, x), fsdp: 4 (over y, core).
Axes of the slice: x: 2, y: 2, z: 4, core: 2. Of those that a mesh axis runs over, the one named last changes fastest.
Arguments:
- tokens: bfloat16 [4, 2048, 8192], P('fsdp', 'ctx'), may hold values from -6 to 6
- queries: bfloat16 [4, 2048, 8192], P('fsdp', 'ctx'), may hold values from -384 to 384
- kv_weight: bfloat16 [8192, 2048], P(None, 'fsdp'), may hold values from -0.0625 to 0.0625
- block_list: int32 [8, 16, 8], replicated, may hold values from 0 to 15, as said below
- counts: int32 [8, 16], replicated, may hold values from 4 to 8, as said below
Outputs:
- attended: bfloat16 [4, 2048, 8192], P('fsdp', 'ctx')
The draws below stay inside these ranges and needn't reach their ends.
Inputs may be any that keep to these rules, and one draw needn't show every extreme that they name: `block_list`: for each g and b the first counts[g, b] entries are distinct: block b, blocks b - 1 and b + 1 modulo 16 (the window wraps at the sequence's ends), the two global blocks of group g, and random blocks; the later entries are further distinct blocks. `counts`: some list has 8 live entries in every draw; loads differ from group to group.
All inputs are finite; a program needn't handle non-finite values.
Results may differ from the reference program's by a relative error of at most 0.007.
The reference program's roundings to bfloat16 on the way (of `keyvals` and `rounded`) count: a program that leaves them out, or rounds other values in their place, can miss the bound.
Values may be sent and summed in bfloat16 or wider, within the bound.
No kernel may reach another device: no remote copies, remote signals or barrier semaphores. Data moves between devices by JAX's collectives and lax.ppermute only.
A program may use at most 192 MiB of HBM per device.

```python
import jax
import jax.numpy as jnp
from jax import lax

D = 8192
HQ = 64
KVH = 8
DH = 128
BLK = 128
RMOST = 3
MAXK = 8
SEQS = 4
LEN = 2048


def draw_queries(key, part):
    normal_part = jnp.clip(jax.random.normal(key, (SEQS, LEN, HQ, DH), jnp.float32), -6.0, 6.0)
    return normal_part.reshape(SEQS, LEN, HQ * DH).astype(jnp.bfloat16)


def block_plan(key):
    blocks = LEN // BLK
    plan_key = jax.random.fold_in(key, 101)
    order_key, global_key, cap_key, chosen_key, extra_key = jax.random.split(plan_key, 5)
    ranking = jax.vmap(lambda sub_key: jax.random.permutation(sub_key, blocks))(jax.random.split(order_key, KVH * blocks))
    ranking = ranking.reshape(KVH, blocks, blocks).astype(jnp.int32)
    global_rank = jax.vmap(lambda sub_key: jax.random.permutation(sub_key, blocks))(jax.random.split(global_key, KVH)).astype(jnp.int32)
    first_global = global_rank[:, 0]
    second_global = global_rank[:, 1]
    column = jnp.arange(blocks, dtype=jnp.int32)
    offset = (column[None, :] - column[:, None]) % blocks
    priority = ranking + 16
    priority = jnp.where(offset[None] == 0, 0, priority)
    priority = jnp.where(offset[None] == blocks - 1, 1, priority)
    priority = jnp.where(offset[None] == 1, 2, priority)
    is_first = column[None, None, :] == first_global[:, None, None]
    priority = jnp.where(is_first, jnp.minimum(priority, 3), priority)
    is_second = column[None, None, :] == second_global[:, None, None]
    priority = jnp.where(is_second, jnp.minimum(priority, 4), priority)
    ordering = jnp.argsort(priority, axis=2)
    picked = ordering[:, :, :MAXK].astype(jnp.int32)
    first_gap = (first_global[:, None] - column[None, :]) % blocks
    second_gap = (second_global[:, None] - column[None, :]) % blocks
    first_inside = ((first_gap == 0) | (first_gap == 1) | (first_gap == blocks - 1)).astype(jnp.int32)
    second_inside = ((second_gap == 0) | (second_gap == 1) | (second_gap == blocks - 1)).astype(jnp.int32)
    window_global = 5 - first_inside - second_inside
    group_ids = jnp.arange(KVH, dtype=jnp.int32)
    busiest = jax.random.randint(chosen_key, (), 0, KVH)
    caps = jax.random.randint(cap_key, (KVH,), 1, RMOST + 1)
    caps = jnp.where(group_ids == busiest, RMOST, caps)
    extra = jax.random.randint(extra_key, (KVH, blocks), 1, caps[:, None] + 1)
    extra = jnp.where(group_ids[:, None] == busiest, RMOST, extra)
    return (picked, (window_global + extra).astype(jnp.int32))


def draw_block_list(key, part):
    return block_plan(key)[0]


def draw_counts(key, part):
    return block_plan(key)[1]


def level_of(key, shape, cuts, low, high):
    factor_of, own = 1.0, jax.random.fold_in(key, 6)
    for axis_at, shards_of in cuts:
        draws = jnp.exp(jax.random.uniform(jax.random.fold_in(own, axis_at), (shards_of,), jnp.float32, low / len(cuts), high / len(cuts)))
        factor_of = factor_of * jnp.repeat(draws, shape[axis_at] // shards_of).reshape([-1 if axis == axis_at else 1 for axis in range(len(shape))])
    return factor_of


def centred(rng, dims, spread, reach, pieces=(), held_as=jnp.bfloat16):
    loudness = level_of(rng, dims, pieces, -0.22, 0.18) if pieces else 1.0
    array = jax.random.normal(rng, dims, jnp.float32) * spread * loudness
    return jnp.minimum(jnp.maximum(array, -reach), reach).astype(held_as)


def setup_inputs(seed: int = 0) -> dict:
    seeds = jax.random.split(jax.random.key(seed), 6)
    return {
        "tokens": centred(seeds[0], (SEQS, LEN, D), 1.0, 6.0, ((0, 4), (1, 8))),
        "queries": draw_queries(jax.random.fold_in(seeds[5], 71), 0),
        "kv_weight": centred(seeds[2], (D, 2 * KVH * DH), D ** -0.5, 0.0625, ((1, 4),)),
        "block_list": draw_block_list(jax.random.fold_in(seeds[5], 71), 0),
        "counts": draw_counts(jax.random.fold_in(seeds[5], 71), 0),
    }


def attend_group(operands):
    query_group, keyval_group, picked, live_count = operands
    blocks = LEN // BLK
    query_blocks = query_group.reshape(blocks, BLK, HQ // KVH, DH).astype(jnp.float32)
    keyval_blocks = keyval_group.reshape(blocks, BLK, 2 * DH)
    chosen = keyval_blocks[picked].astype(jnp.float32).reshape(blocks, MAXK * BLK, 2 * DH)
    key_rows = chosen[:, :, :DH]
    value_rows = chosen[:, :, DH:]
    scores = jnp.einsum("nqhd,nkd->nqhk", query_blocks, key_rows) * (DH ** -0.5)
    slot_index = jnp.arange(MAXK * BLK) // BLK
    live_slot = slot_index[None, :] < live_count[:, None]
    scores = jnp.where(live_slot[:, None, None, :], scores, -jnp.inf)
    row_top = jnp.max(scores, axis=3, keepdims=True)
    weights = jnp.exp(scores - row_top)
    row_total = jnp.sum(weights, axis=3)
    rounded = lax.optimization_barrier(weights.astype(jnp.bfloat16)).astype(jnp.float32)
    weighted = jnp.einsum("nqhk,nkd->nqhd", rounded, value_rows)
    result = (weighted / row_total[..., None]).astype(jnp.bfloat16)
    return result.reshape(LEN, HQ // KVH, DH)


def reference(tokens, queries, kv_weight, block_list, counts):
    outputs = []
    for seq_index in range(SEQS):
        keyvals = jnp.dot(tokens[seq_index], kv_weight, preferred_element_type=jnp.float32).astype(jnp.bfloat16)
        query_group = queries[seq_index].reshape(LEN, KVH, HQ // KVH, DH).transpose(1, 0, 2, 3)
        keyval_group = keyvals.reshape(LEN, KVH, 2 * DH).transpose(1, 0, 2)
        attended = lax.map(attend_group, (query_group, keyval_group, block_list, counts))
        outputs.append(attended.transpose(1, 0, 2, 3).reshape(LEN, HQ * DH))
    return jnp.stack(outputs)
```

```python
import functools

import jax
import jax.numpy as jnp
from jax import lax
from jax.experimental import pallas as pl
from jax.experimental.pallas import tpu as pltpu
from jax.sharding import PartitionSpec as P

DH = 128
BLK = 128
PAIR = 2 * DH
GROUP_HEADS = 8
GROUP_WIDTH = GROUP_HEADS * DH
LOG2E = 1.4426950408889634


def swap(array, axis, bit):
    size = lax.axis_size(axis)
    return lax.ppermute(array, axis, [(i, i ^ bit) for i in range(size)])


def rotate(array, steps):
    pairs = lax.axis_size("ctx") // 2
    order = [(2 * i + m, 2 * ((i + steps) % pairs) + m) for i in range(pairs) for m in range(2)]
    return lax.ppermute(array, "ctx", order)


def gather_pieces(array):
    pairs = lax.axis_size("ctx") // 2
    line = [array] + [rotate(array, r) for r in range(1, pairs)]
    pieces = []
    for piece in line:
        pieces += [piece, swap(piece, "ctx", 1)]
    return pieces


def project(rows, weight):
    return jnp.dot(rows, weight, preferred_element_type=jnp.float32).astype(jnp.bfloat16)


def attend_blocks(live, q_block, key_rows, value_rows, out_ref, row_at):
    scale = DH ** (-0.5) * LOG2E
    for head in range(GROUP_HEADS):
        q = q_block[:, head * DH : (head + 1) * DH]
        scores = lax.dot_general(
            q, key_rows, (((1,), (1,)), ((), ())), preferred_element_type=jnp.float32
        )
        top = jnp.max(scores, axis=1, keepdims=True)
        weights = jnp.exp2((scores - top) * scale)
        total = jnp.sum(weights, axis=1, keepdims=True)
        mixed = jnp.dot(
            weights.astype(jnp.bfloat16), value_rows, preferred_element_type=jnp.float32
        )
        out_ref[pl.ds(row_at, BLK), head * DH : (head + 1) * DH] = (mixed / total).astype(
            jnp.bfloat16
        )


def attend_kernel(
    n_pieces, max_live, group_ref, slot_ref, count_ref, q_ref, *refs
):
    piece_refs = refs[:n_pieces]
    out_ref, held, key_rows, value_rows = refs[-4:]
    step = pl.program_id(0)
    at = 0
    for piece in piece_refs:
        for part in range(piece.shape[0] // BLK):
            held[at] = piece[part * BLK : (part + 1) * BLK, :]
            at += 1
    q_blocks = q_ref.shape[0] // BLK

    def one_block(block, carry):
        row_at = pl.multiple_of(block * BLK, BLK)
        entry = step * q_blocks + block
        count = count_ref[entry]
        for j in range(max_live):
            chosen = held[slot_ref[entry * max_live + j]]
            key_rows[j * BLK : (j + 1) * BLK, :] = chosen[:, :DH]
            value_rows[j * BLK : (j + 1) * BLK, :] = chosen[:, DH:]
        for live in range(4, max_live + 1):

            @pl.when(count == live)
            def _():
                attend_blocks(
                    live,
                    q_ref[pl.ds(row_at, BLK), :],
                    key_rows[: live * BLK, :],
                    value_rows[: live * BLK, :],
                    out_ref,
                    row_at,
                )

        return carry

    lax.fori_loop(0, q_blocks, one_block, 0)


def attend(queries, pieces, groups, slots, counts, so_far):
    n_groups = groups.shape[0]
    rows, width = queries.shape
    max_live = slots.shape[2]
    blocks = sum(p.shape[0] for p in pieces) // BLK
    operands = [groups, slots.reshape(-1), counts.reshape(-1), queries, *pieces]
    in_specs = [pl.BlockSpec((rows, GROUP_WIDTH), lambda i, g, s, c: (0, g[i]))]
    in_specs += [pl.BlockSpec((p.shape[0], PAIR), lambda i, g, s, c: (0, i)) for p in pieces]
    aliases = {}
    if so_far is not None:
        aliases = {len(operands): 0}
        operands.append(so_far)
        in_specs.append(pl.BlockSpec(memory_space=pl.ANY))
    return pl.pallas_call(
        functools.partial(attend_kernel, len(pieces), max_live),
        out_shape=jax.ShapeDtypeStruct((rows, width), jnp.bfloat16),
        grid_spec=pltpu.PrefetchScalarGridSpec(
            num_scalar_prefetch=3,
            grid=(n_groups,),
            in_specs=in_specs,
            out_specs=pl.BlockSpec((rows, GROUP_WIDTH), lambda i, g, s, c: (0, g[i])),
            scratch_shapes=[
                pltpu.VMEM((blocks, BLK, PAIR), jnp.bfloat16),
                pltpu.VMEM((max_live * BLK, DH), jnp.bfloat16),
                pltpu.VMEM((max_live * BLK, DH), jnp.bfloat16),
            ],
        ),
        input_output_aliases=aliases,
        cost_estimate=pl.CostEstimate(
            flops=n_groups * rows * GROUP_WIDTH * max_live * BLK * 4,
            bytes_accessed=n_groups * (blocks * BLK * PAIR + 2 * rows * GROUP_WIDTH) * 2,
            transcendentals=n_groups * rows * GROUP_HEADS * max_live * BLK,
        ),
        compiler_params=pltpu.CompilerParams(vmem_limit_bytes=48 << 20),
    )(*operands)


def on_device(tokens, queries, kv_weight, block_list, counts):
    rows = tokens.shape[1]
    tokens = tokens.reshape(rows, -1)
    queries = queries.reshape(rows, -1)
    n_ctx = lax.axis_size("ctx")
    me, col = lax.axis_index("ctx"), lax.axis_index("fsdp")
    local_blocks = rows // BLK
    local_groups = kv_weight.shape[1] // PAIR
    halves = 2

    half = rows // halves
    sent = [tokens[i * half : (i + 1) * half] for i in range(halves)]
    far = [swap(sent[0], "fsdp", 2)]
    near_weight = swap(kv_weight, "fsdp", 1)

    own = project(tokens, kv_weight)
    own_pieces = gather_pieces(own)
    near = project(tokens, near_weight)
    near_pieces = gather_pieces(near)
    side_weight = (kv_weight, near_weight)
    far_pieces = []
    for i in range(halves):
        got = far[i]
        if i + 1 < halves:
            got, following = lax.optimization_barrier((got, sent[i + 1]))
            far.append(swap(following, "fsdp", 2))
        computed = jnp.concatenate([project(got, w) for w in side_weight], axis=1)
        far_pieces.append(gather_pieces(swap(computed, "fsdp", 2)))

    first = me * local_blocks
    my_list = lax.dynamic_slice_in_dim(block_list, first, local_blocks, 1)
    my_counts = lax.dynamic_slice_in_dim(counts, first, local_blocks, 1)
    source, part = my_list // local_blocks, my_list % local_blocks
    pairs = n_ctx // 2
    piece = 2 * ((me // 2 - source // 2) % pairs) + ((me % 2) ^ (source % 2))
    by_source = piece * local_blocks + part
    by_part = part * n_ctx + piece

    def groups_of(column):
        return column * local_groups + jnp.arange(local_groups, dtype=jnp.int32)

    own_groups, near_groups = groups_of(col), groups_of(col ^ 1)
    far_groups = jnp.concatenate([groups_of(col ^ 2), groups_of(col ^ 3)])
    out = None
    for groups, pieces, slots in (
        (own_groups, own_pieces, by_source),
        (near_groups, near_pieces, by_source),
        (far_groups, far_pieces[0] + far_pieces[1], by_part),
    ):
        out = attend(queries, pieces, groups, slots[groups], my_counts[groups], out)
    return out.reshape(1, rows, -1)


def solution(mesh):
    return jax.shard_map(
        on_device,
        mesh=mesh,
        in_specs=(P("fsdp", "ctx", None), P("fsdp", "ctx", None), P(None, "fsdp"), P(), P()),
        out_specs=P("fsdp", "ctx", None),
        check_vma=False,
    )
```

```python
import functools

import jax
import jax.numpy as jnp
from jax import lax
from jax.experimental import pallas as pl
from jax.experimental.pallas import tpu as pltpu
from jax.sharding import PartitionSpec as P

DH = 128
BLK = 128
PAIR = 2 * DH
GROUP_HEADS = 8
GROUP_WIDTH = GROUP_HEADS * DH
LOG2E = 1.4426950408889634
SHARES = (8, 5, 3)

KERNEL_VMEM = 48 << 20
COST = pl.CostEstimate(flops=1, bytes_accessed=1, transcendentals=0)


def swap(array, axis, bit):
    size = lax.axis_size(axis)
    return lax.ppermute(array, axis, [(i, i ^ bit) for i in range(size)])


def rotate(array, steps, column_bit=0):
    n_ctx, n_col = lax.axis_size("ctx"), lax.axis_size("fsdp")
    order = []
    for c in range(n_ctx):
        to = (c + 2 * steps) % n_ctx
        order += [(c * n_col + f, to * n_col + (f ^ column_bit)) for f in range(n_col)]
    return lax.ppermute(array, ("ctx", "fsdp"), order)


def pin(mark, *arrays):
    return lax.optimization_barrier((mark, *arrays))


def turn_steps():
    pairs = lax.axis_size("ctx") // 2
    return sorted(range(1, pairs), key=lambda r: min(r, pairs - r))


def turn_all(array):
    return [rotate(array, r) for r in turn_steps()]


def cross(array):
    return swap(array, "ctx", 1)


def project_kernel(n_weights, tile, row_ref, *refs):
    weight_refs = refs[:n_weights]
    out_ref, held, total, sems = refs[-4:]
    width = weight_refs[0].shape[1]
    depth = row_ref.shape[1]
    copies = []
    for k in range(depth // tile):
        for i in range(n_weights):
            copies.append(
                pltpu.make_async_copy(
                    weight_refs[i].at[pl.ds(k * tile, tile)],
                    held.at[i, pl.ds(k * tile, tile)],
                    sems.at[k * n_weights + i],
                )
            )
    for copy in copies:
        copy.start()
    for k in range(depth // tile):
        for i in range(n_weights):
            copies[k * n_weights + i].wait()
            product = jnp.dot(
                row_ref[:, k * tile : (k + 1) * tile],
                held[i, k * tile : (k + 1) * tile, :],
                preferred_element_type=jnp.float32,
            )
            columns = slice(i * width, (i + 1) * width)
            if k == 0:
                total[:, columns] = product
            elif k + 1 < depth // tile:
                total[:, columns] += product
            else:
                out_ref[:, columns] = (total[:, columns] + product).astype(jnp.bfloat16)


def project(rows, weights):
    n_rows, depth = rows.shape
    width = weights[0].shape[1]
    tile = 1024
    n_weights = len(weights)
    out_width = width * n_weights
    inside = pl.BlockSpec(memory_space=pltpu.VMEM)
    return pl.pallas_call(
        functools.partial(project_kernel, n_weights, tile),
        out_shape=jax.ShapeDtypeStruct((n_rows, out_width), jnp.bfloat16),
        in_specs=[inside] + [pl.BlockSpec(memory_space=pltpu.HBM)] * n_weights,
        out_specs=inside,
        scratch_shapes=[
            pltpu.VMEM((n_weights, depth, width), jnp.bfloat16),
            pltpu.VMEM((n_rows, out_width), jnp.float32),
            pltpu.SemaphoreType.DMA((depth // tile * n_weights,)),
        ],
        cost_estimate=COST,
        compiler_params=pltpu.CompilerParams(vmem_limit_bytes=KERNEL_VMEM),
    )(rows, *weights)


def attend_blocks(live, q_ref, row_at, state_at, key_rows, value_rows, state_in, results):
    scale = DH ** (-0.5) * LOG2E
    keys = key_rows[: live * BLK, :]
    values = value_rows[: live * BLK, :].astype(jnp.float32).T.astype(jnp.bfloat16)
    for head in range(GROUP_HEADS):
        columns = slice(head * DH, (head + 1) * DH)
        q = q_ref[pl.ds(row_at, BLK), columns]
        scores = lax.dot_general(
            keys, q, (((1,), (1,)), ((), ())), preferred_element_type=jnp.float32
        )
        top = jnp.max(scores, axis=0, keepdims=True)
        weights = jnp.exp2((scores - top) * scale)
        total = jnp.sum(weights, axis=0, keepdims=True)
        mixed = jnp.dot(values, weights.astype(jnp.bfloat16), preferred_element_type=jnp.float32)
        if len(results) == 2:
            results[0][state_at * GROUP_HEADS + head] = mixed
            results[1][state_at * GROUP_HEADS + head, 0:1] = top
            results[1][state_at * GROUP_HEADS + head, 1:2] = total
            continue
        if state_in:
            other = state_in[1][state_at * GROUP_HEADS + head]
            other_top, other_total = other[0:1], other[1:2]
            both = jnp.maximum(top, other_top)
            here, there = jnp.exp2((top - both) * scale), jnp.exp2((other_top - both) * scale)
            total = total * here + other_total * there
            mixed = mixed * here + state_in[0][state_at * GROUP_HEADS + head] * there
        results[0][pl.ds(row_at, BLK), columns] = (mixed / total).T.astype(jnp.bfloat16)


def attend_kernel(places, shape, first_group, part, resumes, group_ref, list_ref, count_ref, me_ref, q_ref, *refs):
    held, q_held, key_rows, value_rows, sems = refs[-5:]
    blocks, max_live, local_blocks = shape
    state_in = refs[len(places) : len(places) + 2] if resumes else ()
    results = refs[-7:-5] if part == 0 else refs[-6:-5]
    held_rows = local_blocks * BLK if part is None else BLK
    pairs = held.shape[1] // (2 * held_rows)
    step, me = pl.program_id(0), me_ref[0]
    n_steps = pl.num_programs(0)

    def copies(index, slot):
        q_at = pl.multiple_of(group_ref[index] * GROUP_WIDTH, GROUP_WIDTH)
        made = [
            pltpu.make_async_copy(
                q_ref.at[:, pl.ds(q_at, GROUP_WIDTH)], q_held.at[slot], sems.at[slot, 0]
            )
        ]
        columns = pl.ds(pl.multiple_of((first_group + index) * PAIR, PAIR), PAIR)
        for ref, place in zip(refs, places):
            at = 0
            for back, member, row_at, rows in place:
                pair = lax.rem(me // 2 + pairs - back, pairs)
                start = pl.multiple_of((2 * pair + member) * held_rows + row_at, 16)
                made.append(
                    pltpu.make_async_copy(
                        ref.at[pl.ds(at, rows), columns],
                        held.at[slot, pl.ds(start, rows)],
                        sems.at[slot, len(made)],
                    )
                )
                at += rows
        return made

    slot = lax.rem(step, 2)

    @pl.when(step == 0)
    def _():
        for copy in copies(step, slot):
            copy.start()

    @pl.when(step + 1 < n_steps)
    def _():
        for copy in copies(step + 1, 1 - slot):
            copy.start()

    for copy in copies(step, slot):
        copy.wait()

    def one_block(block, carry):
        row_at = pl.multiple_of(block * BLK, BLK)
        entry = group_ref[step] * blocks + me * local_blocks + block
        count = count_ref[entry]
        taken = jnp.int32(0)
        for j in range(max_live):
            listed = list_ref[entry * max_live + j]
            source, inside = listed // local_blocks, lax.rem(listed, local_blocks)
            member = lax.rem(source + me, 2)
            from_row = (source // 2 * 2 + member) * held_rows
            wanted = j < count
            if part is None:
                from_row += inside * BLK
            else:
                wanted = jnp.logical_and(wanted, inside == part)
            from_row = pl.multiple_of(from_row, BLK)
            to_row = pl.multiple_of(taken * BLK, BLK)

            @pl.when(wanted)
            def _(from_row=from_row, to_row=to_row):
                chosen = held[slot, pl.ds(from_row, BLK), :]
                key_rows[pl.ds(to_row, BLK), :] = chosen[:, :DH]
                value_rows[pl.ds(to_row, BLK), :] = chosen[:, DH:]

            taken = taken + wanted.astype(jnp.int32)
        for live in range(4, max_live + 1) if part is None else range(1, max_live):
            pl.when(taken == live)(
                functools.partial(
                    attend_blocks,
                    live,
                    q_held.at[slot],
                    row_at,
                    block,
                    key_rows,
                    value_rows,
                    state_in,
                    results,
                )
            )
        return carry

    lax.fori_loop(0, local_blocks, one_block, 0)


def attend(queries, pieces, groups, first_group, block_list, counts, so_far, part=None, state=()):
    n_groups = groups.shape[0]
    rows, width = queries.shape
    local_blocks = rows // BLK
    blocks, max_live = block_list.shape[1:]
    places = [parts for _, parts in pieces]
    held_rows = sum(entry[-1] for parts in places for entry in parts)
    n_copies = 1 + sum(len(parts) for parts in places)
    me = lax.axis_index("ctx").astype(jnp.int32).reshape(1)
    anywhere = pl.BlockSpec(memory_space=pltpu.HBM)
    scalars = [groups, block_list.reshape(-1), counts.reshape(-1), me]
    operands = [queries] + [p for p, _ in pieces]
    in_specs = [anywhere] * len(operands)
    state_shapes = [
        (n_groups * local_blocks * GROUP_HEADS, DH, BLK),
        (n_groups * local_blocks * GROUP_HEADS, 8, BLK),
    ]
    state_specs = [
        pl.BlockSpec((local_blocks * GROUP_HEADS, *shape[1:]), lambda i, *_: (i, 0, 0))
        for shape in state_shapes
    ]
    operands += state
    in_specs += state_specs[: len(state)]
    aliases = {}
    if so_far is not None:
        aliases = {len(scalars) + len(operands): 0}
        operands.append(so_far)
        in_specs.append(anywhere)
    if part == 0:
        out_shape = [jax.ShapeDtypeStruct(shape, jnp.float32) for shape in state_shapes]
        out_specs = state_specs
    else:
        out_shape = jax.ShapeDtypeStruct((rows, width), jnp.bfloat16)
        out_specs = pl.BlockSpec((rows, GROUP_WIDTH), lambda i, g, *_: (0, g[i]))
    return pl.pallas_call(
        functools.partial(
            attend_kernel, places, (blocks, max_live, local_blocks), first_group, part, bool(state)
        ),
        out_shape=out_shape,
        grid_spec=pltpu.PrefetchScalarGridSpec(
            num_scalar_prefetch=len(scalars),
            grid=(n_groups,),
            in_specs=in_specs,
            out_specs=out_specs,
            scratch_shapes=[
                pltpu.VMEM((2, held_rows, PAIR), jnp.bfloat16),
                pltpu.VMEM((2, rows, GROUP_WIDTH), jnp.bfloat16),
                pltpu.VMEM((max_live * BLK, DH), jnp.bfloat16),
                pltpu.VMEM((max_live * BLK, DH), jnp.bfloat16),
                pltpu.SemaphoreType.DMA((2, n_copies)),
            ],
        ),
        input_output_aliases=aliases,
        cost_estimate=COST,
        compiler_params=pltpu.CompilerParams(vmem_limit_bytes=KERNEL_VMEM),
    )(*scalars, *operands)


def on_device(tokens, queries, kv_weight, block_list, counts):
    rows = tokens.shape[1]
    tokens = tokens.reshape(rows, -1)
    queries = queries.reshape(rows, -1)
    col = lax.axis_index("fsdp")
    local_groups = kv_weight.shape[1] // PAIR

    def groups_of(column):
        return column * local_groups + jnp.arange(local_groups, dtype=jnp.int32)

    def attend_to(groups, pieces, half, so_far, part=None, state=()):
        at = half * local_groups
        return attend(queries, pieces, groups, at, block_list, counts, so_far, part, state)

    def line(arrays, backs, place, member):
        return [(p, [(r, member, *place)]) for r, p in zip(backs, arrays)]

    at_second = SHARES[0] * rows // 16
    at_last = (SHARES[0] + SHARES[1]) * rows // 16
    n_turned = at_last - at_second
    steps = turn_steps()
    whole, early = (0, rows), (0, at_second)
    middle, late = (at_second, n_turned), (at_last, rows - at_last)
    pairs = lax.axis_size("ctx") // 2
    mark = jnp.zeros((8, 128), jnp.float32)

    first_got = swap(tokens[:at_second], "fsdp", 2)
    second_out = tokens[at_second:]
    weights = (kv_weight, swap(kv_weight, "fsdp", 1))
    side = project(tokens, weights)

    mark, side, second_out = pin(mark, side, second_out)
    side_turned = [rotate(side, r) for r in steps[:-1]]
    side_crossed = cross(side)
    second_got = swap(second_out, "fsdp", 2)
    mark, side, side_crossed = pin(mark, side, side_crossed)
    side_turned.append(rotate(side, steps[-1]))
    mark, first_got, *side_turned[:-1] = pin(mark, first_got, *side_turned[:-1])
    head_crossed = cross(jnp.concatenate(side_turned[:-1], axis=0))

    first = project(first_got, weights)
    mark, first = pin(mark, first)
    first = rotate(first, 1, 2)
    mark, first, side_turned[-1] = pin(mark, first, side_turned[-1])
    first_turned = turn_all(first)
    first_backs = [(1 + r) % pairs for r in [0, *steps]]
    mark, head_crossed = pin(mark, head_crossed)
    rest_crossed = cross(side_turned[-1])
    mark, rest_crossed, *first_turned = pin(mark, rest_crossed, *first_turned)
    first_crossed = cross(jnp.concatenate([first, *first_turned], axis=0))

    side_pieces = line([side, *side_turned], [0, *steps], whole, 0) + [
        (side_crossed, [(0, 1, *whole)]),
        (head_crossed, [(r, 1, *whole) for r in steps[:-1]]),
        (rest_crossed, [(steps[-1], 1, *whole)]),
    ]
    out = attend_to(groups_of(col), side_pieces, 0, None)
    mark, out, second_got = pin(mark, out, second_got)
    second = project(second_got, weights)
    mark, second = pin(mark, second)
    second = swap(second, "fsdp", 2)
    out = attend_to(groups_of(col ^ 1), side_pieces, 1, out)
    mark, out, second = pin(mark, out, second)

    turned = turn_all(second[:n_turned])
    last_pair = jnp.concatenate([second[n_turned:], cross(second[n_turned:])], axis=0)
    mark, last_pair, *turned = pin(mark, last_pair, *turned)
    crossed = cross(jnp.concatenate([second[:n_turned], *turned], axis=0))
    pair_turned = turn_all(last_pair)

    far_pieces = line([first, *first_turned], first_backs, early, 0)
    far_pieces.append((first_crossed, [(r, 1, *early) for r in first_backs]))
    far_pieces += line([second[:n_turned], *turned], [0, *steps], middle, 0)
    far_pieces.append((crossed, [(r, 1, *middle) for r in [0, *steps]]))
    for r, piece in zip([0, *steps], [last_pair, *pair_turned]):
        far_pieces.append((piece, [(r, 0, *late), (r, 1, *late)]))
    far_groups = jnp.concatenate([groups_of(col ^ 2), groups_of(col ^ 3)])
    out = attend_to(far_groups, far_pieces, 0, out)
    return out.reshape(1, rows, -1)


def solution(mesh):
    return jax.shard_map(
        on_device,
        mesh=mesh,
        in_specs=(P("fsdp", "ctx", None), P("fsdp", "ctx", None), P(None, "fsdp"), P(), P()),
        out_specs=P("fsdp", "ctx", None),
        check_vma=False,
    )
```

```python
import functools

import jax
import jax.numpy as jnp
from jax import lax
from jax.experimental import pallas as pl
from jax.experimental.pallas import tpu as pltpu
from jax.sharding import PartitionSpec as P

DH = 128
BLK = 128
PAIR = 2 * DH
GROUP_HEADS = 8
GROUP_WIDTH = GROUP_HEADS * DH
LOG2E = 1.4426950408889634
SHARES = (8, 5, 3)

KERNEL_VMEM = 48 << 20
COST = pl.CostEstimate(flops=1, bytes_accessed=1, transcendentals=0)


def swap(array, axis, bit):
    size = lax.axis_size(axis)
    return lax.ppermute(array, axis, [(i, i ^ bit) for i in range(size)])


def rotate(array, steps, column_bit=0):
    n_ctx, n_col = lax.axis_size("ctx"), lax.axis_size("fsdp")
    order = []
    for c in range(n_ctx):
        to = (c + 2 * steps) % n_ctx
        order += [(c * n_col + f, to * n_col + (f ^ column_bit)) for f in range(n_col)]
    return lax.ppermute(array, ("ctx", "fsdp"), order)


def pin(mark, *arrays):
    return lax.optimization_barrier((mark, *arrays))


def turn_steps():
    pairs = lax.axis_size("ctx") // 2
    return sorted(range(1, pairs), key=lambda r: -min(r, pairs - r))


def turn_all(array):
    return [rotate(array, r) for r in turn_steps()]


def cross(array):
    return swap(array, "ctx", 1)


def project_kernel(n_weights, tile, row_ref, *refs):
    weight_refs = refs[:n_weights]
    out_ref, held, total, sems = refs[-4:]
    width = weight_refs[0].shape[1]
    depth = row_ref.shape[1]
    copies = []
    for k in range(depth // tile):
        for i in range(n_weights):
            copies.append(
                pltpu.make_async_copy(
                    weight_refs[i].at[pl.ds(k * tile, tile)],
                    held.at[i, pl.ds(k * tile, tile)],
                    sems.at[k * n_weights + i],
                )
            )
    for copy in copies:
        copy.start()
    for k in range(depth // tile):
        for i in range(n_weights):
            copies[k * n_weights + i].wait()
            product = jnp.dot(
                row_ref[:, k * tile : (k + 1) * tile],
                held[i, k * tile : (k + 1) * tile, :],
                preferred_element_type=jnp.float32,
            )
            columns = slice(i * width, (i + 1) * width)
            if k == 0:
                total[:, columns] = product
            elif k + 1 < depth // tile:
                total[:, columns] += product
            else:
                out_ref[:, columns] = (total[:, columns] + product).astype(jnp.bfloat16)


def project(rows, weights):
    n_rows, depth = rows.shape
    width = weights[0].shape[1]
    tile = 1024
    n_weights = len(weights)
    out_width = width * n_weights
    inside = pl.BlockSpec(memory_space=pltpu.VMEM)
    return pl.pallas_call(
        functools.partial(project_kernel, n_weights, tile),
        out_shape=jax.ShapeDtypeStruct((n_rows, out_width), jnp.bfloat16),
        in_specs=[inside] + [pl.BlockSpec(memory_space=pltpu.HBM)] * n_weights,
        out_specs=inside,
        scratch_shapes=[
            pltpu.VMEM((n_weights, depth, width), jnp.bfloat16),
            pltpu.VMEM((n_rows, out_width), jnp.float32),
            pltpu.SemaphoreType.DMA((depth // tile * n_weights,)),
        ],
        cost_estimate=COST,
        compiler_params=pltpu.CompilerParams(vmem_limit_bytes=KERNEL_VMEM),
    )(rows, *weights)


def attend_blocks(live, q_ref, row_at, state_at, key_rows, value_rows, state_in, results):
    scale = DH ** (-0.5) * LOG2E
    keys = key_rows[: live * BLK, :]
    values = value_rows[: live * BLK, :].astype(jnp.float32).T.astype(jnp.bfloat16)
    for head in range(GROUP_HEADS):
        columns = slice(head * DH, (head + 1) * DH)
        q = q_ref[pl.ds(row_at, BLK), columns]
        scores = lax.dot_general(
            keys, q, (((1,), (1,)), ((), ())), preferred_element_type=jnp.float32
        )
        top = jnp.max(scores, axis=0, keepdims=True)
        weights = jnp.exp2((scores - top) * scale)
        total = jnp.sum(weights, axis=0, keepdims=True)
        mixed = jnp.dot(values, weights.astype(jnp.bfloat16), preferred_element_type=jnp.float32)
        if len(results) == 2:
            results[0][state_at * GROUP_HEADS + head] = mixed
            results[1][state_at * GROUP_HEADS + head, 0:1] = top
            results[1][state_at * GROUP_HEADS + head, 1:2] = total
            continue
        if state_in:
            other = state_in[1][state_at * GROUP_HEADS + head]
            other_top, other_total = other[0:1], other[1:2]
            both = jnp.maximum(top, other_top)
            here, there = jnp.exp2((top - both) * scale), jnp.exp2((other_top - both) * scale)
            total = total * here + other_total * there
            mixed = mixed * here + state_in[0][state_at * GROUP_HEADS + head] * there
        results[0][pl.ds(row_at, BLK), columns] = (mixed / total).T.astype(jnp.bfloat16)


def attend_kernel(places, shape, first_group, part, resumes, group_ref, list_ref, count_ref, me_ref, q_ref, *refs):
    held, q_held, key_rows, value_rows, sems = refs[-5:]
    blocks, max_live, local_blocks = shape
    state_in = refs[len(places) : len(places) + 2] if resumes else ()
    results = refs[-7:-5] if part == 0 else refs[-6:-5]
    held_rows = local_blocks * BLK if part is None else BLK
    pairs = held.shape[1] // (2 * held_rows)
    step, me = pl.program_id(0), me_ref[0]
    n_steps = pl.num_programs(0)

    def copies(index, slot):
        q_at = pl.multiple_of(group_ref[index] * GROUP_WIDTH, GROUP_WIDTH)
        made = [
            pltpu.make_async_copy(
                q_ref.at[:, pl.ds(q_at, GROUP_WIDTH)], q_held.at[slot], sems.at[slot, 0]
            )
        ]
        columns = pl.ds(pl.multiple_of((first_group + index) * PAIR, PAIR), PAIR)
        for ref, place in zip(refs, places):
            at = 0
            for back, member, row_at, rows in place:
                pair = lax.rem(me // 2 + pairs - back, pairs)
                start = pl.multiple_of((2 * pair + member) * held_rows + row_at, 16)
                made.append(
                    pltpu.make_async_copy(
                        ref.at[pl.ds(at, rows), columns],
                        held.at[slot, pl.ds(start, rows)],
                        sems.at[slot, len(made)],
                    )
                )
                at += rows
        return made

    slot = lax.rem(step, 2)

    @pl.when(step == 0)
    def _():
        for copy in copies(step, slot):
            copy.start()

    @pl.when(step + 1 < n_steps)
    def _():
        for copy in copies(step + 1, 1 - slot):
            copy.start()

    for copy in copies(step, slot):
        copy.wait()

    def one_block(block, carry):
        row_at = pl.multiple_of(block * BLK, BLK)
        entry = group_ref[step] * blocks + me * local_blocks + block
        count = count_ref[entry]
        taken = jnp.int32(0)
        for j in range(max_live):
            listed = list_ref[entry * max_live + j]
            source, inside = listed // local_blocks, lax.rem(listed, local_blocks)
            member = lax.rem(source + me, 2)
            from_row = (source // 2 * 2 + member) * held_rows
            wanted = j < count
            if part is None:
                from_row += inside * BLK
            else:
                wanted = jnp.logical_and(wanted, inside == part)
            from_row = pl.multiple_of(from_row, BLK)
            to_row = pl.multiple_of(taken * BLK, BLK)

            @pl.when(wanted)
            def _(from_row=from_row, to_row=to_row):
                chosen = held[slot, pl.ds(from_row, BLK), :]
                key_rows[pl.ds(to_row, BLK), :] = chosen[:, :DH]
                value_rows[pl.ds(to_row, BLK), :] = chosen[:, DH:]

            taken = taken + wanted.astype(jnp.int32)
        for live in range(4, max_live + 1) if part is None else range(1, max_live):
            pl.when(taken == live)(
                functools.partial(
                    attend_blocks,
                    live,
                    q_held.at[slot],
                    row_at,
                    block,
                    key_rows,
                    value_rows,
                    state_in,
                    results,
                )
            )
        return carry

    lax.fori_loop(0, local_blocks, one_block, 0)


def attend(queries, pieces, groups, first_group, block_list, counts, so_far, part=None, state=()):
    n_groups = groups.shape[0]
    rows, width = queries.shape
    local_blocks = rows // BLK
    blocks, max_live = block_list.shape[1:]
    places = [parts for _, parts in pieces]
    held_rows = sum(entry[-1] for parts in places for entry in parts)
    n_copies = 1 + sum(len(parts) for parts in places)
    me = lax.axis_index("ctx").astype(jnp.int32).reshape(1)
    anywhere = pl.BlockSpec(memory_space=pltpu.HBM)
    scalars = [groups, block_list.reshape(-1), counts.reshape(-1), me]
    operands = [queries] + [p for p, _ in pieces]
    in_specs = [anywhere] * len(operands)
    state_shapes = [
        (n_groups * local_blocks * GROUP_HEADS, DH, BLK),
        (n_groups * local_blocks * GROUP_HEADS, 8, BLK),
    ]
    state_specs = [
        pl.BlockSpec((local_blocks * GROUP_HEADS, *shape[1:]), lambda i, *_: (i, 0, 0))
        for shape in state_shapes
    ]
    operands += state
    in_specs += state_specs[: len(state)]
    aliases = {}
    if so_far is not None:
        aliases = {len(scalars) + len(operands): 0}
        operands.append(so_far)
        in_specs.append(anywhere)
    if part == 0:
        out_shape = [jax.ShapeDtypeStruct(shape, jnp.float32) for shape in state_shapes]
        out_specs = state_specs
    else:
        out_shape = jax.ShapeDtypeStruct((rows, width), jnp.bfloat16)
        out_specs = pl.BlockSpec((rows, GROUP_WIDTH), lambda i, g, *_: (0, g[i]))
    return pl.pallas_call(
        functools.partial(
            attend_kernel, places, (blocks, max_live, local_blocks), first_group, part, bool(state)
        ),
        out_shape=out_shape,
        grid_spec=pltpu.PrefetchScalarGridSpec(
            num_scalar_prefetch=len(scalars),
            grid=(n_groups,),
            in_specs=in_specs,
            out_specs=out_specs,
            scratch_shapes=[
                pltpu.VMEM((2, held_rows, PAIR), jnp.bfloat16),
                pltpu.VMEM((2, rows, GROUP_WIDTH), jnp.bfloat16),
                pltpu.VMEM((max_live * BLK, DH), jnp.bfloat16),
                pltpu.VMEM((max_live * BLK, DH), jnp.bfloat16),
                pltpu.SemaphoreType.DMA((2, n_copies)),
            ],
        ),
        input_output_aliases=aliases,
        cost_estimate=COST,
        compiler_params=pltpu.CompilerParams(vmem_limit_bytes=60 << 20),
    )(*scalars, *operands)


def on_device(tokens, queries, kv_weight, block_list, counts):
    rows = tokens.shape[1]
    tokens = tokens.reshape(rows, -1)
    queries = queries.reshape(rows, -1)
    col = lax.axis_index("fsdp")
    local_groups = kv_weight.shape[1] // PAIR

    def groups_of(column):
        return column * local_groups + jnp.arange(local_groups, dtype=jnp.int32)

    def attend_to(groups, pieces, half, so_far, part=None, state=()):
        at = half * local_groups
        return attend(queries, pieces, groups, at, block_list, counts, so_far, part, state)

    def line(arrays, backs, place, member):
        return [(p, [(r, member, *place)]) for r, p in zip(backs, arrays)]

    at_second = SHARES[0] * rows // 16
    at_last = (SHARES[0] + SHARES[1]) * rows // 16
    n_turned = at_last - at_second
    steps = turn_steps()
    whole, early = (0, rows), (0, at_second)
    middle, late = (0, n_turned), (n_turned, rows - at_last)
    pairs = lax.axis_size("ctx") // 2
    mark = jnp.zeros((8, 128), jnp.float32)

    first_got = swap(tokens[:at_second], "fsdp", 2)
    second_out = tokens[at_second:]
    near_weight = swap(kv_weight, "fsdp", 1)
    own = project(tokens, (kv_weight,))

    mark, own, second_out = pin(mark, own, second_out)
    own_turned = turn_all(own)
    near = project(tokens, (near_weight,))
    mark, near, *own_turned = pin(mark, near, *own_turned)
    own_line = [own, *own_turned]
    own_crossed = cross(jnp.concatenate(own_line, axis=0))
    near_turned = turn_all(near)
    second_got = swap(second_out, "fsdp", 2)
    mark, first_got = pin(mark, first_got)

    def side_pieces(pieces, crossed):
        return line(pieces, [0, *steps], whole, 0) + [(crossed, [(r, 1, *whole) for r in [0, *steps]])]

    first = project(first_got, (kv_weight, near_weight))
    mark, first, own_crossed, *near_turned = pin(mark, first, own_crossed, *near_turned)
    first = rotate(first, 1, 2)
    near_line = [near, *near_turned]
    near_crossed = cross(jnp.concatenate(near_line, axis=0))
    mark, first = pin(mark, first)
    first_turned = turn_all(first)
    first_backs = [(1 + r) % pairs for r in [0, *steps]]
    out = attend_to(groups_of(col), side_pieces(own_line, own_crossed), 0, None)

    mark, out, near_crossed, second_got, *first_turned = pin(
        mark, out, near_crossed, second_got, *first_turned
    )
    first_crossed = cross(jnp.concatenate([first, *first_turned], axis=0))
    second = project(second_got, (kv_weight, near_weight))
    mark, second = pin(mark, second)
    back = swap(second, "fsdp", 2)
    turned = [rotate(second[:n_turned], r, 2) for r in steps]
    out = attend_to(groups_of(col ^ 1), side_pieces(near_line, near_crossed), 0, out)
    mark, out, back = pin(mark, out, back)
    last_crossed = cross(back[n_turned:])

    mark, last_crossed, first_crossed, *turned = pin(mark, last_crossed, first_crossed, *turned)
    crossed = cross(jnp.concatenate([back[:n_turned], *turned], axis=0))
    last_pair = jnp.concatenate([back[n_turned:], last_crossed], axis=0)
    pair_turned = turn_all(last_pair)

    far_groups = jnp.concatenate([groups_of(col ^ 2), groups_of(col ^ 3)])
    first_pieces = line([first, *first_turned], first_backs, early, 0)
    first_pieces.append((first_crossed, [(r, 1, *early) for r in first_backs]))
    state = attend_to(far_groups, first_pieces, 0, None, 0)
    mark, crossed, *rest = pin(mark, crossed, *pair_turned, *state)
    pair_turned, state = rest[: len(steps)], rest[len(steps) :]

    second_pieces = line([back[:n_turned], *turned], [0, *steps], middle, 0)
    second_pieces.append((crossed, [(r, 1, *middle) for r in [0, *steps]]))
    for r, piece in zip([0, *steps], [last_pair, *pair_turned]):
        second_pieces.append((piece, [(r, 0, *late), (r, 1, *late)]))
    out = attend_to(far_groups, second_pieces, 0, out, 1, state)
    return out.reshape(1, rows, -1)


def solution(mesh):
    return jax.shard_map(
        on_device,
        mesh=mesh,
        in_specs=(P("fsdp", "ctx", None), P("fsdp", "ctx", None), P(None, "fsdp"), P(), P()),
        out_specs=P("fsdp", "ctx", None),
        check_vma=False,
    )
```

```python
import functools

import jax
import jax.numpy as jnp
from jax import lax
from jax.experimental import pallas as pl
from jax.experimental.pallas import tpu as pltpu
from jax.sharding import PartitionSpec as P

DH = 128
BLK = 128
PAIR = 2 * DH
GROUP_HEADS = 8
GROUP_WIDTH = GROUP_HEADS * DH
LOG2E = 1.4426950408889634
SHARES = (8, 5, 3)

KERNEL_VMEM = 48 << 20
COST = pl.CostEstimate(flops=1, bytes_accessed=1, transcendentals=0)


def swap(array, axis, bit):
    size = lax.axis_size(axis)
    return lax.ppermute(array, axis, [(i, i ^ bit) for i in range(size)])


def rotate(array, steps, column_bit=0):
    n_ctx, n_col = lax.axis_size("ctx"), lax.axis_size("fsdp")
    order = []
    for c in range(n_ctx):
        to = (c + 2 * steps) % n_ctx
        order += [(c * n_col + f, to * n_col + (f ^ column_bit)) for f in range(n_col)]
    return lax.ppermute(array, ("ctx", "fsdp"), order)


def pin(mark, *arrays):
    return lax.optimization_barrier((mark, *arrays))


def cut_kernel(start, in_ref, out_ref, sem):
    copy = pltpu.make_async_copy(in_ref.at[pl.ds(start, out_ref.shape[0])], out_ref, sem)
    copy.start()
    copy.wait()


def cut(array, start, rows):
    return pl.pallas_call(
        functools.partial(cut_kernel, start),
        out_shape=jax.ShapeDtypeStruct((rows, array.shape[1]), array.dtype),
        in_specs=[pl.BlockSpec(memory_space=pltpu.HBM)],
        out_specs=pl.BlockSpec(memory_space=pltpu.VMEM),
        scratch_shapes=[pltpu.SemaphoreType.DMA],
        cost_estimate=COST,
        compiler_params=pltpu.CompilerParams(vmem_limit_bytes=8 << 20),
    )(array)


def turn_steps():
    pairs = lax.axis_size("ctx") // 2
    return sorted(range(1, pairs), key=lambda r: min(r, pairs - r))


def turn_all(array):
    return [rotate(array, r) for r in turn_steps()]


def cross(array):
    return swap(array, "ctx", 1)


def project_kernel(n_weights, tile, row_ref, *refs):
    weight_refs = refs[:n_weights]
    out_ref, held, total, sems = refs[-4:]
    width = weight_refs[0].shape[1]
    depth = row_ref.shape[1]
    copies = []
    for k in range(depth // tile):
        for i in range(n_weights):
            copies.append(
                pltpu.make_async_copy(
                    weight_refs[i].at[pl.ds(k * tile, tile)],
                    held.at[i, pl.ds(k * tile, tile)],
                    sems.at[k * n_weights + i],
                )
            )
    for copy in copies:
        copy.start()
    for k in range(depth // tile):
        for i in range(n_weights):
            copies[k * n_weights + i].wait()
            product = jnp.dot(
                row_ref[:, k * tile : (k + 1) * tile],
                held[i, k * tile : (k + 1) * tile, :],
                preferred_element_type=jnp.float32,
            )
            columns = slice(i * width, (i + 1) * width)
            if k == 0:
                total[:, columns] = product
            elif k + 1 < depth // tile:
                total[:, columns] += product
            else:
                out_ref[:, columns] = (total[:, columns] + product).astype(jnp.bfloat16)


def project(rows, weights):
    n_rows, depth = rows.shape
    width = weights[0].shape[1]
    tile = 1024
    n_weights = len(weights)
    out_width = width * n_weights
    inside = pl.BlockSpec(memory_space=pltpu.VMEM)
    return pl.pallas_call(
        functools.partial(project_kernel, n_weights, tile),
        out_shape=jax.ShapeDtypeStruct((n_rows, out_width), jnp.bfloat16),
        in_specs=[inside] + [pl.BlockSpec(memory_space=pltpu.HBM)] * n_weights,
        out_specs=inside,
        scratch_shapes=[
            pltpu.VMEM((n_weights, depth, width), jnp.bfloat16),
            pltpu.VMEM((n_rows, out_width), jnp.float32),
            pltpu.SemaphoreType.DMA((depth // tile * n_weights,)),
        ],
        cost_estimate=COST,
        compiler_params=pltpu.CompilerParams(vmem_limit_bytes=KERNEL_VMEM),
    )(rows, *weights)


def attend_blocks(live, q_ref, row_at, state_at, key_rows, value_rows, state_in, results):
    scale = DH ** (-0.5) * LOG2E
    keys = key_rows[: live * BLK, :]
    values = value_rows[: live * BLK, :].astype(jnp.float32).T.astype(jnp.bfloat16)
    for head in range(GROUP_HEADS):
        columns = slice(head * DH, (head + 1) * DH)
        q = q_ref[pl.ds(row_at, BLK), columns]
        scores = lax.dot_general(
            keys, q, (((1,), (1,)), ((), ())), preferred_element_type=jnp.float32
        )
        top = jnp.max(scores, axis=0, keepdims=True)
        weights = jnp.exp2((scores - top) * scale)
        total = jnp.sum(weights, axis=0, keepdims=True)
        mixed = jnp.dot(values, weights.astype(jnp.bfloat16), preferred_element_type=jnp.float32)
        if len(results) == 2:
            results[0][state_at * GROUP_HEADS + head] = mixed
            results[1][state_at * GROUP_HEADS + head, 0:1] = top
            results[1][state_at * GROUP_HEADS + head, 1:2] = total
            continue
        if state_in:
            other = state_in[1][state_at * GROUP_HEADS + head]
            other_top, other_total = other[0:1], other[1:2]
            both = jnp.maximum(top, other_top)
            here, there = jnp.exp2((top - both) * scale), jnp.exp2((other_top - both) * scale)
            total = total * here + other_total * there
            mixed = mixed * here + state_in[0][state_at * GROUP_HEADS + head] * there
        results[0][pl.ds(row_at, BLK), columns] = (mixed / total).T.astype(jnp.bfloat16)


def attend_kernel(places, shape, first_group, part, resumes, group_ref, list_ref, count_ref, me_ref, q_ref, *refs):
    held, q_held, key_rows, value_rows, sems = refs[-5:]
    blocks, max_live, local_blocks = shape
    state_in = refs[len(places) : len(places) + 2] if resumes else ()
    results = refs[-7:-5] if part == 0 else refs[-6:-5]
    held_rows = local_blocks * BLK if part is None else BLK
    pairs = held.shape[1] // (2 * held_rows)
    step, me = pl.program_id(0), me_ref[0]
    n_steps = pl.num_programs(0)

    def copies(index, slot):
        q_at = pl.multiple_of(group_ref[index] * GROUP_WIDTH, GROUP_WIDTH)
        made = [
            pltpu.make_async_copy(
                q_ref.at[:, pl.ds(q_at, GROUP_WIDTH)], q_held.at[slot], sems.at[slot, 0]
            )
        ]
        columns = pl.ds(pl.multiple_of((first_group + index) * PAIR, PAIR), PAIR)
        for ref, place in zip(refs, places):
            at = 0
            for back, member, row_at, rows in place:
                pair = lax.rem(me // 2 + pairs - back, pairs)
                start = pl.multiple_of((2 * pair + member) * held_rows + row_at, 16)
                made.append(
                    pltpu.make_async_copy(
                        ref.at[pl.ds(at, rows), columns],
                        held.at[slot, pl.ds(start, rows)],
                        sems.at[slot, len(made)],
                    )
                )
                at += rows
        return made

    slot = lax.rem(step, 2)

    @pl.when(step == 0)
    def _():
        for copy in copies(step, slot):
            copy.start()

    @pl.when(step + 1 < n_steps)
    def _():
        for copy in copies(step + 1, 1 - slot):
            copy.start()

    for copy in copies(step, slot):
        copy.wait()

    def one_block(block, carry):
        row_at = pl.multiple_of(block * BLK, BLK)
        entry = group_ref[step] * blocks + me * local_blocks + block
        count = count_ref[entry]
        taken = jnp.int32(0)
        for j in range(max_live):
            listed = list_ref[entry * max_live + j]
            source, inside = listed // local_blocks, lax.rem(listed, local_blocks)
            member = lax.rem(source + me, 2)
            from_row = (source // 2 * 2 + member) * held_rows
            wanted = j < count
            if part is None:
                from_row += inside * BLK
            else:
                wanted = jnp.logical_and(wanted, inside == part)
            from_row = pl.multiple_of(from_row, BLK)
            to_row = pl.multiple_of(taken * BLK, BLK)

            @pl.when(wanted)
            def _(from_row=from_row, to_row=to_row):
                chosen = held[slot, pl.ds(from_row, BLK), :]
                key_rows[pl.ds(to_row, BLK), :] = chosen[:, :DH]
                value_rows[pl.ds(to_row, BLK), :] = chosen[:, DH:]

            taken = taken + wanted.astype(jnp.int32)
        for live in range(4, max_live + 1) if part is None else range(1, max_live):
            pl.when(taken == live)(
                functools.partial(
                    attend_blocks,
                    live,
                    q_held.at[slot],
                    row_at,
                    block,
                    key_rows,
                    value_rows,
                    state_in,
                    results,
                )
            )
        return carry

    lax.fori_loop(0, local_blocks, one_block, 0)


def attend(queries, pieces, groups, first_group, block_list, counts, so_far, part=None, state=()):
    n_groups = groups.shape[0]
    rows, width = queries.shape
    local_blocks = rows // BLK
    blocks, max_live = block_list.shape[1:]
    places = [parts for _, parts in pieces]
    held_rows = sum(entry[-1] for parts in places for entry in parts)
    n_copies = 1 + sum(len(parts) for parts in places)
    me = lax.axis_index("ctx").astype(jnp.int32).reshape(1)
    anywhere = pl.BlockSpec(memory_space=pltpu.HBM)
    scalars = [groups, block_list.reshape(-1), counts.reshape(-1), me]
    operands = [queries] + [p for p, _ in pieces]
    in_specs = [anywhere] * len(operands)
    state_shapes = [
        (n_groups * local_blocks * GROUP_HEADS, DH, BLK),
        (n_groups * local_blocks * GROUP_HEADS, 8, BLK),
    ]
    state_specs = [
        pl.BlockSpec((local_blocks * GROUP_HEADS, *shape[1:]), lambda i, *_: (i, 0, 0))
        for shape in state_shapes
    ]
    operands += state
    in_specs += state_specs[: len(state)]
    aliases = {}
    if so_far is not None:
        aliases = {len(scalars) + len(operands): 0}
        operands.append(so_far)
        in_specs.append(anywhere)
    if part == 0:
        out_shape = [jax.ShapeDtypeStruct(shape, jnp.float32) for shape in state_shapes]
        out_specs = state_specs
    else:
        out_shape = jax.ShapeDtypeStruct((rows, width), jnp.bfloat16)
        out_specs = pl.BlockSpec((rows, GROUP_WIDTH), lambda i, g, *_: (0, g[i]))
    return pl.pallas_call(
        functools.partial(
            attend_kernel, places, (blocks, max_live, local_blocks), first_group, part, bool(state)
        ),
        out_shape=out_shape,
        grid_spec=pltpu.PrefetchScalarGridSpec(
            num_scalar_prefetch=len(scalars),
            grid=(n_groups,),
            in_specs=in_specs,
            out_specs=out_specs,
            scratch_shapes=[
                pltpu.VMEM((2, held_rows, PAIR), jnp.bfloat16),
                pltpu.VMEM((2, rows, GROUP_WIDTH), jnp.bfloat16),
                pltpu.VMEM((max_live * BLK, DH), jnp.bfloat16),
                pltpu.VMEM((max_live * BLK, DH), jnp.bfloat16),
                pltpu.SemaphoreType.DMA((2, n_copies)),
            ],
        ),
        input_output_aliases=aliases,
        cost_estimate=COST,
        compiler_params=pltpu.CompilerParams(vmem_limit_bytes=60 << 20),
    )(*scalars, *operands)


def on_device(tokens, queries, kv_weight, block_list, counts):
    rows = tokens.shape[1]
    tokens = tokens.reshape(rows, -1)
    queries = queries.reshape(rows, -1)
    col = lax.axis_index("fsdp")
    local_groups = kv_weight.shape[1] // PAIR

    def groups_of(column):
        return column * local_groups + jnp.arange(local_groups, dtype=jnp.int32)

    def attend_to(groups, pieces, half, so_far, part=None, state=()):
        at = half * local_groups
        return attend(queries, pieces, groups, at, block_list, counts, so_far, part, state)

    def line(arrays, backs, place, member):
        return [(p, [(r, member, *place)]) for r, p in zip(backs, arrays)]

    at_second = SHARES[0] * rows // 16
    at_last = (SHARES[0] + SHARES[1]) * rows // 16
    n_turned = at_last - at_second
    steps = turn_steps()
    whole, early = (0, rows), (0, at_second)
    middle, late = (at_second, n_turned), (at_last, rows - at_last)
    pairs = lax.axis_size("ctx") // 2
    mark = jnp.zeros((8, 128), jnp.float32)

    first_got = swap(cut(tokens, 0, at_second), "fsdp", 2)
    second_out = tokens[at_second:]
    near_weight = swap(kv_weight, "fsdp", 1)
    own = project(tokens, (kv_weight,))

    mark, own, second_out = pin(mark, own, second_out)
    own_turned = turn_all(own)
    near = project(tokens, (near_weight,))
    mark, near, *own_turned = pin(mark, near, *own_turned)
    own_line = [own, *own_turned]
    own_crossed = cross(jnp.concatenate(own_line, axis=0))
    near_turned = turn_all(near)
    second_got = swap(second_out, "fsdp", 2)
    mark, first_got, own_crossed = pin(mark, first_got, own_crossed)

    def side_pieces(pieces, crossed):
        return line(pieces, [0, *steps], whole, 0) + [(crossed, [(r, 1, *whole) for r in [0, *steps]])]

    first = project(first_got, (kv_weight, near_weight))
    mark, first, *near_turned = pin(mark, first, *near_turned)
    first = rotate(first, 1, 2)
    near_line = [near, *near_turned]
    near_crossed = cross(jnp.concatenate(near_line, axis=0))
    mark, first = pin(mark, first)
    first_turned = turn_all(first)
    first_backs = [(1 + r) % pairs for r in [0, *steps]]
    out = attend_to(groups_of(col), side_pieces(own_line, own_crossed), 0, None)

    mark, out, near_crossed, *first_turned = pin(mark, out, near_crossed, *first_turned)
    first_crossed = cross(jnp.concatenate([first, *first_turned], axis=0))
    mark, second_got = pin(mark, second_got)
    second = project(second_got, (kv_weight, near_weight))
    mark, second = pin(mark, second)
    back = swap(second, "fsdp", 2)
    turned = [rotate(second[:n_turned], r, 2) for r in steps]
    mark, back = pin(mark, back)
    last_crossed = cross(back[n_turned:])

    mark, last_crossed, first_crossed, *turned = pin(mark, last_crossed, first_crossed, *turned)
    crossed = cross(jnp.concatenate([back[:n_turned], *turned], axis=0))
    last_pair = jnp.concatenate([back[n_turned:], last_crossed], axis=0)
    pair_turned = turn_all(last_pair)

    out = attend_to(groups_of(col ^ 1), side_pieces(near_line, near_crossed), 0, out)
    mark, out, crossed, *pair_turned = pin(mark, out, crossed, *pair_turned)

    far_pieces = line([first, *first_turned], first_backs, early, 0)
    far_pieces.append((first_crossed, [(r, 1, *early) for r in first_backs]))
    far_pieces += line([back[:n_turned], *turned], [0, *steps], middle, 0)
    far_pieces.append((crossed, [(r, 1, *middle) for r in [0, *steps]]))
    for r, piece in zip([0, *steps], [last_pair, *pair_turned]):
        far_pieces.append((piece, [(r, 0, *late), (r, 1, *late)]))
    far_groups = jnp.concatenate([groups_of(col ^ 2), groups_of(col ^ 3)])
    out = attend_to(far_groups, far_pieces, 0, out)
    return out.reshape(1, rows, -1)


def solution(mesh):
    return jax.shard_map(
        on_device,
        mesh=mesh,
        in_specs=(P("fsdp", "ctx", None), P("fsdp", "ctx", None), P(None, "fsdp"), P(), P()),
        out_specs=P("fsdp", "ctx", None),
        check_vma=False,
    )
```

```python
import functools

import jax
import jax.numpy as jnp
from jax import lax
from jax.experimental import pallas as pl
from jax.experimental.pallas import tpu as pltpu
from jax.sharding import PartitionSpec as P

DH = 128
BLK = 128
PAIR = 2 * DH
GROUP_HEADS = 8
GROUP_WIDTH = GROUP_HEADS * DH
LOG2E = 1.4426950408889634
SHARES = (8, 5, 3)

KERNEL_VMEM = 48 << 20
COST = pl.CostEstimate(flops=1, bytes_accessed=1, transcendentals=0)


def swap(array, axis, bit):
    size = lax.axis_size(axis)
    return lax.ppermute(array, axis, [(i, i ^ bit) for i in range(size)])


def rotate(array, steps, column_bit=0):
    n_ctx, n_col = lax.axis_size("ctx"), lax.axis_size("fsdp")
    order = []
    for c in range(n_ctx):
        to = (c + 2 * steps) % n_ctx
        order += [(c * n_col + f, to * n_col + (f ^ column_bit)) for f in range(n_col)]
    return lax.ppermute(array, ("ctx", "fsdp"), order)


def pin(mark, *arrays):
    return lax.optimization_barrier((mark, *arrays))


def cut_kernel(start, in_ref, out_ref, sem):
    copy = pltpu.make_async_copy(in_ref.at[pl.ds(start, out_ref.shape[0])], out_ref, sem)
    copy.start()
    copy.wait()


def cut(array, start, rows):
    return pl.pallas_call(
        functools.partial(cut_kernel, start),
        out_shape=jax.ShapeDtypeStruct((rows, array.shape[1]), array.dtype),
        in_specs=[pl.BlockSpec(memory_space=pltpu.HBM)],
        out_specs=pl.BlockSpec(memory_space=pltpu.VMEM),
        scratch_shapes=[pltpu.SemaphoreType.DMA],
        cost_estimate=COST,
        compiler_params=pltpu.CompilerParams(vmem_limit_bytes=8 << 20),
    )(array)


def turn_steps():
    pairs = lax.axis_size("ctx") // 2
    return sorted(range(1, pairs), key=lambda r: min(r, pairs - r))


def turn_all(array):
    return [rotate(array, r) for r in turn_steps()]


def cross(array):
    return swap(array, "ctx", 1)


def project_kernel(n_weights, tile, row_ref, *refs):
    weight_refs = refs[:n_weights]
    out_ref, held, total, sems = refs[-4:]
    width = weight_refs[0].shape[1]
    depth = row_ref.shape[1]
    copies = []
    for k in range(depth // tile):
        for i in range(n_weights):
            copies.append(
                pltpu.make_async_copy(
                    weight_refs[i].at[pl.ds(k * tile, tile)],
                    held.at[i, pl.ds(k * tile, tile)],
                    sems.at[k * n_weights + i],
                )
            )
    for copy in copies:
        copy.start()
    for k in range(depth // tile):
        for i in range(n_weights):
            copies[k * n_weights + i].wait()
            product = jnp.dot(
                row_ref[:, k * tile : (k + 1) * tile],
                held[i, k * tile : (k + 1) * tile, :],
                preferred_element_type=jnp.float32,
            )
            columns = slice(i * width, (i + 1) * width)
            if k == 0:
                total[:, columns] = product
            elif k + 1 < depth // tile:
                total[:, columns] += product
            else:
                out_ref[:, columns] = (total[:, columns] + product).astype(jnp.bfloat16)


def project(rows, weights):
    n_rows, depth = rows.shape
    width = weights[0].shape[1]
    tile = 1024
    n_weights = len(weights)
    out_width = width * n_weights
    inside = pl.BlockSpec(memory_space=pltpu.VMEM)
    return pl.pallas_call(
        functools.partial(project_kernel, n_weights, tile),
        out_shape=jax.ShapeDtypeStruct((n_rows, out_width), jnp.bfloat16),
        in_specs=[inside] + [pl.BlockSpec(memory_space=pltpu.HBM)] * n_weights,
        out_specs=inside,
        scratch_shapes=[
            pltpu.VMEM((n_weights, depth, width), jnp.bfloat16),
            pltpu.VMEM((n_rows, out_width), jnp.float32),
            pltpu.SemaphoreType.DMA((depth // tile * n_weights,)),
        ],
        cost_estimate=COST,
        compiler_params=pltpu.CompilerParams(vmem_limit_bytes=KERNEL_VMEM),
    )(rows, *weights)


def attend_blocks(live, q_ref, row_at, state_at, key_rows, value_rows, state_in, results):
    scale = DH ** (-0.5) * LOG2E
    keys = key_rows[: live * BLK, :]
    values = value_rows[: live * BLK, :].astype(jnp.float32).T.astype(jnp.bfloat16)
    for head in range(GROUP_HEADS):
        columns = slice(head * DH, (head + 1) * DH)
        q = q_ref[pl.ds(row_at, BLK), columns]
        scores = lax.dot_general(
            keys, q, (((1,), (1,)), ((), ())), preferred_element_type=jnp.float32
        )
        top = jnp.max(scores, axis=0, keepdims=True)
        weights = jnp.exp2((scores - top) * scale)
        total = jnp.sum(weights, axis=0, keepdims=True)
        mixed = jnp.dot(values, weights.astype(jnp.bfloat16), preferred_element_type=jnp.float32)
        if len(results) == 2:
            results[0][state_at * GROUP_HEADS + head] = mixed
            results[1][state_at * GROUP_HEADS + head, 0:1] = top
            results[1][state_at * GROUP_HEADS + head, 1:2] = total
            continue
        if state_in:
            other = state_in[1][state_at * GROUP_HEADS + head]
            other_top, other_total = other[0:1], other[1:2]
            both = jnp.maximum(top, other_top)
            here, there = jnp.exp2((top - both) * scale), jnp.exp2((other_top - both) * scale)
            total = total * here + other_total * there
            mixed = mixed * here + state_in[0][state_at * GROUP_HEADS + head] * there
        results[0][pl.ds(row_at, BLK), columns] = (mixed / total).T.astype(jnp.bfloat16)


def attend_kernel(places, shape, first_group, part, resumes, group_ref, list_ref, count_ref, me_ref, q_ref, *refs):
    held, q_held, key_rows, value_rows, sems = refs[-5:]
    blocks, max_live, local_blocks = shape
    state_in = refs[len(places) : len(places) + 2] if resumes else ()
    results = refs[-7:-5] if part == 0 else refs[-6:-5]
    held_rows = local_blocks * BLK if part is None else BLK
    pairs = held.shape[1] // (2 * held_rows)
    step, me = pl.program_id(0), me_ref[0]
    n_steps = pl.num_programs(0)

    def copies(index, slot):
        q_at = pl.multiple_of(group_ref[index] * GROUP_WIDTH, GROUP_WIDTH)
        made = [
            pltpu.make_async_copy(
                q_ref.at[:, pl.ds(q_at, GROUP_WIDTH)], q_held.at[slot], sems.at[slot, 0]
            )
        ]
        columns = pl.ds(pl.multiple_of((first_group + index) * PAIR, PAIR), PAIR)
        for ref, place in zip(refs, places):
            at = 0
            for back, member, row_at, rows in place:
                pair = lax.rem(me // 2 + pairs - back, pairs)
                start = pl.multiple_of((2 * pair + member) * held_rows + row_at, 16)
                made.append(
                    pltpu.make_async_copy(
                        ref.at[pl.ds(at, rows), columns],
                        held.at[slot, pl.ds(start, rows)],
                        sems.at[slot, len(made)],
                    )
                )
                at += rows
        return made

    slot = lax.rem(step, 2)

    @pl.when(step == 0)
    def _():
        for copy in copies(step, slot):
            copy.start()

    @pl.when(step + 1 < n_steps)
    def _():
        for copy in copies(step + 1, 1 - slot):
            copy.start()

    for copy in copies(step, slot):
        copy.wait()

    def one_block(block, carry):
        row_at = pl.multiple_of(block * BLK, BLK)
        entry = group_ref[step] * blocks + me * local_blocks + block
        count = count_ref[entry]
        taken = jnp.int32(0)
        for j in range(max_live):
            listed = list_ref[entry * max_live + j]
            source, inside = listed // local_blocks, lax.rem(listed, local_blocks)
            member = lax.rem(source + me, 2)
            from_row = (source // 2 * 2 + member) * held_rows
            wanted = j < count
            if part is None:
                from_row += inside * BLK
            else:
                wanted = jnp.logical_and(wanted, inside == part)
            from_row = pl.multiple_of(from_row, BLK)
            to_row = pl.multiple_of(taken * BLK, BLK)

            @pl.when(wanted)
            def _(from_row=from_row, to_row=to_row):
                chosen = held[slot, pl.ds(from_row, BLK), :]
                key_rows[pl.ds(to_row, BLK), :] = chosen[:, :DH]
                value_rows[pl.ds(to_row, BLK), :] = chosen[:, DH:]

            taken = taken + wanted.astype(jnp.int32)
        for live in range(4, max_live + 1) if part is None else range(1, max_live):
            pl.when(taken == live)(
                functools.partial(
                    attend_blocks,
                    live,
                    q_held.at[slot],
                    row_at,
                    block,
                    key_rows,
                    value_rows,
                    state_in,
                    results,
                )
            )
        return carry

    lax.fori_loop(0, local_blocks, one_block, 0)


def attend(queries, pieces, groups, first_group, block_list, counts, so_far, part=None, state=()):
    n_groups = groups.shape[0]
    rows, width = queries.shape
    local_blocks = rows // BLK
    blocks, max_live = block_list.shape[1:]
    places = [parts for _, parts in pieces]
    held_rows = sum(entry[-1] for parts in places for entry in parts)
    n_copies = 1 + sum(len(parts) for parts in places)
    me = lax.axis_index("ctx").astype(jnp.int32).reshape(1)
    anywhere = pl.BlockSpec(memory_space=pltpu.HBM)
    scalars = [groups, block_list.reshape(-1), counts.reshape(-1), me]
    operands = [queries] + [p for p, _ in pieces]
    in_specs = [anywhere] * len(operands)
    state_shapes = [
        (n_groups * local_blocks * GROUP_HEADS, DH, BLK),
        (n_groups * local_blocks * GROUP_HEADS, 8, BLK),
    ]
    state_specs = [
        pl.BlockSpec((local_blocks * GROUP_HEADS, *shape[1:]), lambda i, *_: (i, 0, 0))
        for shape in state_shapes
    ]
    operands += state
    in_specs += state_specs[: len(state)]
    aliases = {}
    if so_far is not None:
        aliases = {len(scalars) + len(operands): 0}
        operands.append(so_far)
        in_specs.append(anywhere)
    if part == 0:
        out_shape = [jax.ShapeDtypeStruct(shape, jnp.float32) for shape in state_shapes]
        out_specs = state_specs
    else:
        out_shape = jax.ShapeDtypeStruct((rows, width), jnp.bfloat16)
        out_specs = pl.BlockSpec((rows, GROUP_WIDTH), lambda i, g, *_: (0, g[i]))
    return pl.pallas_call(
        functools.partial(
            attend_kernel, places, (blocks, max_live, local_blocks), first_group, part, bool(state)
        ),
        out_shape=out_shape,
        grid_spec=pltpu.PrefetchScalarGridSpec(
            num_scalar_prefetch=len(scalars),
            grid=(n_groups,),
            in_specs=in_specs,
            out_specs=out_specs,
            scratch_shapes=[
                pltpu.VMEM((2, held_rows, PAIR), jnp.bfloat16),
                pltpu.VMEM((2, rows, GROUP_WIDTH), jnp.bfloat16),
                pltpu.VMEM((max_live * BLK, DH), jnp.bfloat16),
                pltpu.VMEM((max_live * BLK, DH), jnp.bfloat16),
                pltpu.SemaphoreType.DMA((2, n_copies)),
            ],
        ),
        input_output_aliases=aliases,
        cost_estimate=COST,
        compiler_params=pltpu.CompilerParams(vmem_limit_bytes=60 << 20),
    )(*scalars, *operands)


def on_device(tokens, queries, kv_weight, block_list, counts):
    rows = tokens.shape[1]
    tokens = tokens.reshape(rows, -1)
    queries = queries.reshape(rows, -1)
    col = lax.axis_index("fsdp")
    local_groups = kv_weight.shape[1] // PAIR

    def groups_of(column):
        return column * local_groups + jnp.arange(local_groups, dtype=jnp.int32)

    def attend_to(groups, pieces, half, so_far, part=None, state=()):
        at = half * local_groups
        return attend(queries, pieces, groups, at, block_list, counts, so_far, part, state)

    def line(arrays, backs, place, member):
        return [(p, [(r, member, *place)]) for r, p in zip(backs, arrays)]

    at_second = SHARES[0] * rows // 16
    at_last = (SHARES[0] + SHARES[1]) * rows // 16
    n_turned = at_last - at_second
    steps = turn_steps()
    whole, early = (0, rows), (0, at_second)
    middle, late = (at_second, n_turned), (at_last, rows - at_last)
    pairs = lax.axis_size("ctx") // 2
    mark = jnp.zeros((8, 128), jnp.float32)

    first_got = swap(cut(tokens, 0, at_second), "fsdp", 2)
    second_out = tokens[at_second:]
    near_weight = swap(kv_weight, "fsdp", 1)
    own = project(tokens, (kv_weight,))

    mark, own, second_out = pin(mark, own, second_out)
    own_turned = turn_all(own)
    near = project(tokens, (near_weight,))
    mark, near, *own_turned = pin(mark, near, *own_turned)
    own_line = [own, *own_turned]
    own_crossed = cross(jnp.concatenate(own_line, axis=0))
    near_turned = turn_all(near)
    second_got = swap(second_out, "fsdp", 2)
    mark, first_got = pin(mark, first_got)

    def side_pieces(pieces, crossed):
        return line(pieces, [0, *steps], whole, 0) + [(crossed, [(r, 1, *whole) for r in [0, *steps]])]

    first = project(first_got, (kv_weight, near_weight))
    mark, first, own_crossed, *near_turned = pin(mark, first, own_crossed, *near_turned)
    first = rotate(first, 1, 2)
    near_line = [near, *near_turned]
    near_crossed = cross(jnp.concatenate(near_line, axis=0))
    mark, first = pin(mark, first)
    first_turned = turn_all(first)
    first_backs = [(1 + r) % pairs for r in [0, *steps]]
    out = attend_to(groups_of(col), side_pieces(own_line, own_crossed), 0, None)

    mark, out, near_crossed, *first_turned = pin(mark, out, near_crossed, *first_turned)
    first_crossed = cross(jnp.concatenate([first, *first_turned], axis=0))
    mark, second_got = pin(mark, second_got)
    second = project(second_got, (kv_weight, near_weight))
    mark, second = pin(mark, second)
    back = swap(second, "fsdp", 2)
    turned = [rotate(second[:n_turned], r, 2) for r in steps]
    mark, back = pin(mark, back)
    last_crossed = cross(back[n_turned:])

    mark, last_crossed, first_crossed, *turned = pin(mark, last_crossed, first_crossed, *turned)
    crossed = cross(jnp.concatenate([back[:n_turned], *turned], axis=0))
    last_pair = jnp.concatenate([back[n_turned:], last_crossed], axis=0)
    pair_turned = turn_all(last_pair)

    out = attend_to(groups_of(col ^ 1), side_pieces(near_line, near_crossed), 0, out)
    mark, out, crossed, *pair_turned = pin(mark, out, crossed, *pair_turned)

    far_pieces = line([first, *first_turned], first_backs, early, 0)
    far_pieces.append((first_crossed, [(r, 1, *early) for r in first_backs]))
    far_pieces += line([back[:n_turned], *turned], [0, *steps], middle, 0)
    far_pieces.append((crossed, [(r, 1, *middle) for r in [0, *steps]]))
    for r, piece in zip([0, *steps], [last_pair, *pair_turned]):
        far_pieces.append((piece, [(r, 0, *late), (r, 1, *late)]))
    far_groups = jnp.concatenate([groups_of(col ^ 2), groups_of(col ^ 3)])
    out = attend_to(far_groups, far_pieces, 0, out)
    return out.reshape(1, rows, -1)


def solution(mesh):
    return jax.shard_map(
        on_device,
        mesh=mesh,
        in_specs=(P("fsdp", "ctx", None), P("fsdp", "ctx", None), P(None, "fsdp"), P(), P()),
        out_specs=P("fsdp", "ctx", None),
        check_vma=False,
    )
```
